32 devices in a mesh: dp: 2 (over x), expert: 16 (over z, y, core).
Axes of the slice: x: 2, y: 2, z: 4, core: 2. Of those that a mesh axis runs over, the one named last changes fastest.
Arguments:
- tokens: bfloat16 [512, 2048], P(('dp', 'expert')), may hold values from -6 to 6
- routes: int32 [512, 8], P(('dp', 'expert')), may hold values from 0 to 15, all different within a row; in each aligned block of 16 rows (0 to 15, 16 to 31, ...) at most 16 rows name the same one
- gates: float32 [512, 8], P(('dp', 'expert')), may hold values from 0.02 to 0.5
- cotangent: bfloat16 [512, 2048], P(('dp', 'expert')), may hold values from -6 to 6
- w_gate: bfloat16 [16, 2048, 768], P('expert', 'dp'), may hold values from -0.125 to 0.125
- w_up: bfloat16 [16, 2048, 768], P('expert', 'dp'), may hold values from -0.125 to 0.125
- w_down: bfloat16 [16, 768, 2048], P('expert', None, 'dp'), may hold values from -0.21875 to 0.21875
Outputs:
- layer_out: bfloat16 [512, 2048], P(('dp', 'expert'))
- d_tokens: bfloat16 [512, 2048], P(('dp', 'expert'))
- grad_gate: bfloat16 [16, 2048, 768], P('expert', 'dp')
- grad_up: bfloat16 [16, 2048, 768], P('expert', 'dp')
- grad_down: bfloat16 [16, 768, 2048], P('expert', None, 'dp')
The draws below stay inside these ranges and needn't reach their ends.
Inputs may be any that keep to these rules, and one draw needn't show every extreme that they name: `routes`: each token names 8 different experts. Among the 16 tokens of one device (aligned blocks of token rows) no expert is named by more than 16 tokens, a bound that some block reaches.
All inputs are finite; a program needn't handle non-finite values.
Results may differ from the reference program's by a relative error of at most 0.019.
Values may be sent and summed in bfloat16 or wider, within the bound.
No kernel may reach another device: no remote copies, remote signals or barrier semaphores. Data moves between devices by JAX's collectives and lax.ppermute only.
A program may use at most 64 MiB of HBM per device.

```python
import math
import jax
import jax.numpy as jnp
import numpy as np
from jax import lax

D = 2048
FF = 768
TOP = 8
TOK_DEV = 16
EXPERTS = 16
CAP = 16
DQ = 1024
TOKENS = 512
N_DP = 2


def block_levels(own_key, extent, shards, least, top_value):
    loudness, own = 1.0, jax.random.fold_in(own_key, 6)
    for dim, blocks in shards:
        steps = jnp.exp(jax.random.uniform(jax.random.fold_in(own, dim), (blocks,), jnp.float32, least / len(shards), top_value / len(shards)))
        loudness = loudness * jnp.repeat(steps, extent[dim] // blocks).reshape([-1 if axis == dim else 1 for axis in range(len(extent))])
    return loudness


def shared_out(own_key, own, number, rows, count, top, limit, lean):
    order = jax.random.permutation(own_key, count)
    heavy_load, common = portions_of(count, rows * top, limit, lean, True), portions_of(count, rows * top, limit, lean, False)
    places = jnp.arange(count)

    def named(tallies, turn):
        used = int((tallies > 0).sum())
        fixed = max(1, used // 4)
        moved = fixed + (places - fixed + turn * (used - fixed)) % max(1, count - fixed)
        return jnp.zeros((count,), jnp.int32).at[order[jnp.where(places < fixed, places, moved)]].set(jnp.asarray(tallies, jnp.int32))

    tallies = jnp.where(number % 4 == 0, named(heavy_load, number // 4), named(common, number - number // 4 - 1))
    mixed = jax.random.permutation(jax.random.fold_in(own, 3), count)
    giver, taker = mixed[0:count // 2 * 2:2], mixed[1:count // 2 * 2:2]
    slack = jnp.minimum(tallies[giver] - 1, limit - tallies[taker]) // 2
    slack = jnp.where((giver == order[0]) | (taker == order[0]) | (tallies[taker] == 0), 0, jnp.maximum(slack, 0))
    moved = jax.random.randint(jax.random.fold_in(own, 4), (count // 2,), 0, 1 << 20) % (slack + 1)
    tallies = tallies.at[giver].add(-moved).at[taker].add(moved)
    members = jnp.searchsorted(jnp.cumsum(tallies), jnp.arange(rows * top), side="right").astype(jnp.int32)
    table = members.reshape(top, rows).T
    table = table[jax.random.permutation(jax.random.fold_in(own, 1), rows)]
    turn = jax.random.randint(jax.random.fold_in(own, 2), (rows, 1), 0, top)
    return jnp.take_along_axis(table, (jnp.arange(top)[None, :] + turn) % top, axis=1)


def portions_of(count, total, most, lean, full):
    weights = [(1 << 20) // math.isqrt(grade ** lean) + 1 for grade in range(1, count + 1)]
    largest = most if full else min(most, max(-(-total // count), total * weights[0] // sum(weights)))
    least = 1 if total - largest >= count - 1 else 0
    holding, surplus = [largest] + [least] * (count - 1), total - largest - least * (count - 1)
    while surplus > 0:
        free = [i for i in range(1, count) if holding[i] < largest] or [i for i in range(1, count) if holding[i] < most]
        pool, left = sum([weights[i] for i in free]), surplus
        for i in free:
            addition = min(most - holding[i], max(1, left * weights[i] // pool), surplus)
            holding[i] = holding[i] + addition
            surplus = surplus - addition
    return np.array(holding)


def noise(key, dims, width, bound, shards=(), held_as=jnp.bfloat16):
    values = width * jax.random.normal(key, dims, jnp.float32)
    if shards:
        values = values * block_levels(key, dims, shards, -0.22, 0.18)
    return jnp.clip(values, -bound, bound).astype(held_as)


def setup_inputs(seed: int = 0) -> dict:
    streams_of = jax.random.split(jax.random.key(seed), 8)
    tokens = noise(streams_of[0], (TOKENS, D), 1.0, 6.0, ((0, 32),))
    routes_keys = jax.random.split(jax.random.fold_in(streams_of[1], 1), TOKENS // TOK_DEV)
    routes_turns = jax.random.permutation(jax.random.fold_in(streams_of[1], 3), TOKENS // TOK_DEV)
    routes = jax.vmap(lambda own, number: shared_out(jax.random.fold_in(streams_of[1], 2), own, number, TOK_DEV, EXPERTS, TOP, CAP, 2))(routes_keys, routes_turns).reshape((TOKENS, TOP))
    gates = jnp.clip(jnp.exp(math.log(0.5) - 3.218876 * jax.random.uniform(streams_of[2], (TOKENS, TOP), jnp.float32) ** block_levels(streams_of[2], (TOKENS, TOP), ((0, 32),), -0.2, 0.2)), 0.02, 0.5)
    cotangent = noise(streams_of[3], (TOKENS, D), 1.0, 6.0, ((0, 32),))
    w_gate = noise(streams_of[4], (EXPERTS, D, FF), D ** -0.5, 0.125, ((0, 16), (1, 2)))
    w_up = noise(streams_of[5], (EXPERTS, D, FF), D ** -0.5, 0.125, ((0, 16), (1, 2)))
    w_down = noise(streams_of[6], (EXPERTS, FF, D), FF ** -0.5, 0.21875, ((0, 16), (2, 2)))
    return {"tokens": tokens, "routes": routes, "gates": gates, "cotangent": cotangent, "w_gate": w_gate, "w_up": w_up, "w_down": w_down}


def part_sum(left, weight_parts, form):
    pieces = jnp.einsum(form, left, weight_parts)
    pieces = lax.optimization_barrier(pieces.astype(jnp.bfloat16))
    return jnp.sum(pieces.astype(jnp.float32), axis=0)


def reference(tokens, routes, gates, cotangent, w_gate, w_up, w_down):
    sources = TOKENS // TOK_DEV
    assigned = TOK_DEV * TOP
    slot_rows = sources * CAP
    expert_ids = routes.reshape(sources, assigned)
    expert_iota = jnp.arange(EXPERTS, dtype=jnp.int32)
    onehot = (expert_ids[:, :, None] == expert_iota[None, None, :]).astype(jnp.int32)
    prior_count = jnp.cumsum(onehot, axis=1) - onehot
    slot_index = jnp.sum(prior_count * onehot, axis=2).astype(jnp.int32)
    source_iota = jnp.arange(sources, dtype=jnp.int32)[:, None]
    flat_pos = (expert_ids * slot_rows + source_iota * CAP + slot_index).reshape(-1)
    labels = (jnp.arange(sources * assigned, dtype=jnp.int32) + 1).astype(jnp.int32)
    table = jnp.zeros((EXPERTS * slot_rows,), jnp.int32).at[flat_pos].set(labels)
    table = table.reshape(EXPERTS, slot_rows)
    gate_flat = gates.reshape(-1)

    def per_expert(carry, inputs):
        out_acc, grad_acc = carry
        labels_here, gate_w, up_w, down_w = inputs
        valid = labels_here > 0
        assign_index = jnp.maximum(labels_here - 1, 0).astype(jnp.int32)
        token_index = (assign_index // TOP).astype(jnp.int32)
        input_rows = jnp.where(valid[:, None], tokens[token_index], jnp.zeros((), jnp.bfloat16)).astype(jnp.bfloat16)
        gate_rows = jnp.where(valid, gate_flat[assign_index], jnp.zeros((), jnp.float32))
        dout_rows = (gate_rows[:, None] * cotangent[token_index].astype(jnp.float32)).astype(jnp.bfloat16)
        left_parts = input_rows.astype(jnp.float32).reshape(slot_rows, N_DP, DQ)
        gate_pre = part_sum(left_parts, gate_w.astype(jnp.float32).reshape(N_DP, DQ, FF), "rqd,qdf->qrf")
        up_pre = part_sum(left_parts, up_w.astype(jnp.float32).reshape(N_DP, DQ, FF), "rqd,qdf->qrf")
        sigmoid_gate = jax.nn.sigmoid(gate_pre)
        silu_gate = gate_pre * sigmoid_gate
        hidden = (silu_gate * up_pre).astype(jnp.bfloat16)
        expert_out = jnp.dot(hidden, down_w, preferred_element_type=jnp.float32).astype(jnp.bfloat16)
        dout_parts = dout_rows.astype(jnp.float32).reshape(slot_rows, N_DP, DQ)
        d_hidden = part_sum(dout_parts, down_w.astype(jnp.float32).reshape(FF, N_DP, DQ), "rqd,fqd->qrf")
        d_gate_pre = (d_hidden * up_pre * sigmoid_gate * (1.0 + gate_pre * (1.0 - sigmoid_gate))).astype(jnp.bfloat16)
        d_up_pre = (d_hidden * silu_gate).astype(jnp.bfloat16)
        grad_down = jnp.einsum("rf,rd->fd", hidden.astype(jnp.float32), dout_rows.astype(jnp.float32)).astype(jnp.bfloat16)
        grad_gate = jnp.einsum("rd,rf->df", input_rows.astype(jnp.float32), d_gate_pre.astype(jnp.float32)).astype(jnp.bfloat16)
        grad_up = jnp.einsum("rd,rf->df", input_rows.astype(jnp.float32), d_up_pre.astype(jnp.float32)).astype(jnp.bfloat16)
        d_assign = (jnp.einsum("rf,df->rd", d_gate_pre.astype(jnp.float32), gate_w.astype(jnp.float32))
                    + jnp.einsum("rf,df->rd", d_up_pre.astype(jnp.float32), up_w.astype(jnp.float32))).astype(jnp.bfloat16)
        out_terms = jnp.where(valid[:, None], gate_rows[:, None] * expert_out.astype(jnp.float32), jnp.zeros((), jnp.float32))
        grad_terms = jnp.where(valid[:, None], d_assign.astype(jnp.float32), jnp.zeros((), jnp.float32))
        out_acc = out_acc.at[token_index].add(out_terms)
        grad_acc = grad_acc.at[token_index].add(grad_terms)
        return (out_acc, grad_acc), (grad_gate, grad_up, grad_down)

    start = (jnp.zeros((TOKENS, D), jnp.float32), jnp.zeros((TOKENS, D), jnp.float32))
    (out_acc, grad_acc), (grad_gate, grad_up, grad_down) = lax.scan(per_expert, start, (table, w_gate, w_up, w_down))
    return out_acc.astype(jnp.bfloat16), grad_acc.astype(jnp.bfloat16), grad_gate, grad_up, grad_down
```

```python
import functools

import jax
import jax.numpy as jnp
from jax import lax
from jax.experimental import pallas as pl
from jax.experimental.pallas import tpu as pltpu
from jax.sharding import PartitionSpec as P


def swap(value, dp_bit, expert_bits):
    groups, experts = lax.axis_size("dp"), lax.axis_size("expert")
    if dp_bit == 0:
        pairs = [(e, e ^ expert_bits) for e in range(experts)]
        return lax.ppermute(value, "expert", pairs)
    pairs = [
        (d * experts + e, (d ^ dp_bit) * experts + (e ^ expert_bits))
        for d in range(groups)
        for e in range(experts)
    ]
    return lax.ppermute(value, ("dp", "expert"), pairs)


def prepare_kernel(tokens_ref, routes_ref, gates_ref, cotangent_ref, mine_ref, other_ref, *, experts, part):
    rows, fanout = tokens_ref.shape[0], routes_ref.shape[0]
    width = mine_ref.shape[1] - 2 * part
    routes, gates = routes_ref[...].T, gates_ref[...].T
    lane = lax.broadcasted_iota(jnp.int32, (rows, width), 1)
    named = lax.rem(lane, experts)
    table = jnp.zeros((rows, width), jnp.float32)
    for k in range(fanout):
        table = table + jnp.where(routes[:, k : k + 1] == named, gates[:, k : k + 1], 0.0)
    high = table.astype(jnp.bfloat16).astype(jnp.float32)
    middle = (table - high).astype(jnp.bfloat16).astype(jnp.float32)
    low = table - high - middle
    piece = lane // experts
    extra = jnp.where(piece == 0, high, jnp.where(piece == 1, middle, jnp.where(piece == 2, low, 0.0)))
    extra = extra.astype(jnp.bfloat16)
    dp_index = lax.axis_index("dp")
    for ref, owner in ((mine_ref, dp_index), (other_ref, 1 - dp_index)):
        columns = pl.ds(pl.multiple_of(owner * part, part), part)
        ref[:, :part] = tokens_ref[:, columns]
        ref[:, part : 2 * part] = cotangent_ref[:, columns]
        ref[:, 2 * part :] = extra


def begin(copies):
    for copy in copies:
        copy.start()
    return copies


def partial_kernel(count, parts, experts, part, *refs):
    f32, bf16 = jnp.float32, jnp.bfloat16
    pieces, weights = refs[:count], refs[count : count + 3]
    scale_ref, input_ref, dout_ref = refs[-3:]
    own_refs = refs[-3 - parts : -3]
    gate_ref, up_ref, down_ref = (weight.at[0] for weight in weights)
    units = gate_ref.shape[1]
    start = 0
    for piece in pieces:
        rows = piece.shape[0]
        here = slice(start, start + rows)
        start += rows
        extra = piece[:, 2 * part :].astype(f32)
        lane = lax.broadcasted_iota(jnp.int32, extra.shape, 1)
        scale = jnp.sum(
            jnp.where(lax.rem(lane, experts) == lax.axis_index("expert"), extra, 0.0), axis=1, keepdims=True
        )
        scale_ref[here, :] = jnp.broadcast_to(scale, (rows, scale_ref.shape[1]))
        input_ref[here, :] = piece[:, :part]
        dout_ref[here, :] = (scale * piece[:, part : 2 * part].astype(f32)).astype(bf16)
    def store(columns, value):
        start = 0
        for ref in own_refs:
            ref[:, columns] = value[start : start + ref.shape[0]].astype(bf16)
            start += ref.shape[0]

    for i, weight in enumerate((gate_ref, up_ref)):
        store(
            slice(i * units, (i + 1) * units),
            jnp.dot(input_ref[...], weight[...], preferred_element_type=f32),
        )
    across = (((1,), (1,)), ((), ()))
    store(
        slice(2 * units, 3 * units),
        lax.dot_general(dout_ref[...], down_ref[...], across, preferred_element_type=f32),
    )


def expert_kernel(block, skipped, parts, first, own_ref, their_ref, scale_ref, *refs):
    f32, bf16 = jnp.float32, jnp.bfloat16
    weights, refs = refs[:3], refs[3 + skipped :]
    pieces, refs = refs[:parts], refs[parts:]
    hidden_ref, dgate_ref, dup_ref = refs
    gate_ref, up_ref, down_ref = (weight.at[0] for weight in weights)
    rows = own_ref.shape[0]
    part, units = gate_ref.shape
    blocks = [their_ref[(i ^ 1) * block : ((i ^ 1) + 1) * block, :] for i in range(rows // block)]
    total = own_ref[...].astype(f32) + jnp.concatenate(blocks, axis=0).astype(f32)
    gate, up, dhidden = total[:, :units], total[:, units : 2 * units], total[:, 2 * units :]
    sigmoid = jax.nn.sigmoid(gate)
    silu = gate * sigmoid
    hidden_ref[...] = (silu * up).astype(bf16)
    dgate_ref[...] = (dhidden * up * sigmoid * (1.0 + gate * (1.0 - sigmoid))).astype(bf16)
    dup_ref[...] = (dhidden * silu).astype(bf16)
    half = rows // parts
    out = scale_ref[first : first + rows, :1] * jnp.dot(hidden_ref[...], down_ref[...], preferred_element_type=f32)
    for i, ref in enumerate(pieces):
        ref[:, :part] = out[i * half : (i + 1) * half].astype(bf16)
    across = (((1,), (1,)), ((), ()))
    back = lax.dot_general(dgate_ref[...], gate_ref[...], across, preferred_element_type=f32)
    back = back + lax.dot_general(dup_ref[...], up_ref[...], across, preferred_element_type=f32)
    for i, ref in enumerate(pieces):
        ref[:, part:] = back[i * half : (i + 1) * half].astype(bf16)


def merge_kernel(count, parts, *refs):
    terms, pieces = refs[:count], refs[-parts:]
    start = 0
    for piece in pieces:
        rows = piece.shape[0]
        total = sum(term[start : start + rows, :].astype(jnp.float32) for term in terms)
        piece[...] = total.astype(piece.dtype)
        start += rows


def gather_kernel(count, *refs):
    start = 0
    for piece in refs[:count]:
        refs[-1][start : start + piece.shape[0], :] = piece[...]
        start += piece.shape[0]


def finish_kernel(count, *refs):
    f32 = jnp.float32
    out_ref, back_ref = refs[2 * count :]
    part = refs[0].shape[1] // 2
    dp_index = lax.axis_index("dp")
    for owner, terms in ((dp_index, refs[:count]), (1 - dp_index, refs[count : 2 * count])):
        columns = pl.ds(pl.multiple_of(owner * part, part), part)
        for ref, start in ((out_ref, 0), (back_ref, part)):
            total = sum(term[:, start : start + part].astype(f32) for term in terms)
            ref[:, columns] = total.astype(ref.dtype)


def grad_kernel(counts, *refs):
    bf16 = jnp.bfloat16
    groups, start = [], 0
    for count in counts:
        groups.append(refs[start : start + count])
        start += count
    outs, results, done = refs[-7:-4], refs[-4:-1], refs[-1]

    def rows_of(group):
        return jnp.concatenate([ref[...] for ref in group], axis=0)

    over_rows = (((0,), (0,)), ((), ()))
    copies = []
    for i, (left, right) in enumerate(((0, 3), (0, 4), (2, 1))):
        results[i][0] = lax.dot_general(
            rows_of(groups[left]),
            rows_of(groups[right]),
            over_rows,
            preferred_element_type=jnp.float32,
        ).astype(bf16)
        copies += begin([pltpu.make_async_copy(results[i], outs[i], done.at[i])])
    for copy in copies:
        copy.wait()


def dense(tokens, routes, gates, cotangent, w_gate, w_up, w_down):
    f32, bf16 = jnp.float32, jnp.bfloat16
    rows, features = tokens.shape
    experts = lax.axis_size("expert")
    part, units = w_gate.shape[1:]
    wide = 2 * part + -(-3 * experts // 128) * 128
    params = pltpu.CompilerParams(vmem_limit_bytes=20 * 1024 * 1024)
    largest = pltpu.CompilerParams(vmem_limit_bytes=52 * 1024 * 1024)
    little = pltpu.CompilerParams(vmem_limit_bytes=4 * 1024 * 1024)
    long = pl.CostEstimate(flops=int(1e10), bytes_accessed=1000, transcendentals=0)
    small = pl.CostEstimate(flops=1000, bytes_accessed=1000, transcendentals=0)
    vmem = pl.BlockSpec(memory_space=pltpu.VMEM)
    anywhere = pl.BlockSpec(memory_space=pl.ANY)
    hbm = pl.BlockSpec(memory_space=pltpu.HBM)

    def shape(*dims, dtype=bf16):
        return jax.ShapeDtypeStruct(dims, dtype)

    mine, other = pl.pallas_call(
        functools.partial(prepare_kernel, experts=experts, part=part),
        out_shape=(shape(rows, wide), shape(rows, wide)),
        in_specs=[vmem] * 4,
        out_specs=(vmem, vmem),
        cost_estimate=long,
        compiler_params=params,
        name="prepare",
    )(tokens, routes.T, gates.T, cotangent)

    weights = (w_gate, w_up, w_down)
    busy = pl.CostEstimate(flops=int(1e3), bytes_accessed=1000, transcendentals=0)

    last, kept = [], []

    def partials(pieces, sizes):
        nonlocal last
        count = sum(piece.shape[0] for piece in pieces)
        outs = pl.pallas_call(
            functools.partial(partial_kernel, len(pieces), len(sizes), experts, part),
            out_shape=tuple(shape(size, 3 * units) for size in sizes)
            + (shape(count, 128, dtype=f32), shape(count, part), shape(count, part)),
            in_specs=[vmem] * len(pieces) + [vmem] * (3 + len(last)),
            out_specs=(vmem,) * (len(sizes) + 3),
            cost_estimate=busy,
            compiler_params=params,
            name="partials",
        )(*pieces, *weights, *last)
        last = [outs[len(sizes)]]
        return outs[: len(sizes)], outs[-3:]

    def expert(own, theirs, scale, first, parts):
        nonlocal last
        count = own.shape[0]
        outs = pl.pallas_call(
            functools.partial(expert_kernel, rows, len(last), parts, first),
            out_shape=(shape(count // parts, 2 * part),) * parts + (shape(count, units),) * 3,
            in_specs=[vmem] * 3 + [vmem] * (3 + len(last)),
            out_specs=(vmem,) * (parts + 3),
            cost_estimate=busy,
            compiler_params=params,
            name="expert",
        )(own, theirs, scale, *weights, *last)
        last = [outs[0]]
        return outs[:parts], outs[parts:]

    def merge(terms, sizes):
        nonlocal last
        outs = pl.pallas_call(
            functools.partial(merge_kernel, len(terms), len(sizes)),
            out_shape=tuple(shape(size, terms[0].shape[1]) for size in sizes),
            in_specs=[vmem] * (len(terms) + len(last)),
            out_specs=(vmem,) * len(sizes),
            cost_estimate=small,
            compiler_params=little,
            name="merge",
        )(*terms, *last)
        last = [outs[0]]
        return list(outs)

    def gather(pieces):
        nonlocal last
        out = pl.pallas_call(
            functools.partial(gather_kernel, len(pieces)),
            out_shape=shape(sum(piece.shape[0] for piece in pieces), pieces[0].shape[1]),
            in_specs=[vmem] * (len(pieces) + len(last)),
            out_specs=vmem,
            cost_estimate=small if last else long,
            compiler_params=little,
            name="gather",
        )(*pieces, *last)
        last = [out]
        return out

    order = [4 * z for z in [0, 1] + list(range(experts // 4 - 1, 1, -1))]
    steps = len(order)
    quads = [gather([mine, swap(other, 1, 0), swap(mine, 0, 2), swap(other, 1, 2)])]
    quads += [swap(quads[0], 0, bits) for bits in order[1:]]
    sent, saved, near = {}, [], None

    def project(k):
        quad = gather([quads[k]]) if k > 1 else quads[k]
        pieces = [quad, swap(quad, 0, 1)]
        [own], (scale, *rest) = partials(pieces, [8 * rows])
        sent[k] = (own, swap(own, 1, 0), scale)
        kept.append(rest)

    def act(k):
        (keep, send), rest = expert(*sent[k], 0, 2)
        saved.append(rest)
        return [keep, swap(send, 0, 1)]

    project(0)
    project(1)
    sums = []
    for k in range(steps):
        terms = act(k)
        if k + 2 < steps:
            relay = gather([quads[k + 2]])
            across = swap(relay, 0, 1)
        if k >= 2:
            near = merge([near, sums[k - 1]], [4 * rows] if k < steps - 1 else [rows] * 4)
            near = near[0] if k < steps - 1 else near
        if k == steps - 1:
            close = merge(terms, [rows] * 4)
            break
        [total] = merge(terms, [4 * rows])
        if k == 0:
            near = total
        sums.append(swap(total, 0, order[k]) if k else total)
        if k + 2 < steps:
            [own], (scale, *rest) = partials([relay, across], [8 * rows])
            sent[k + 2] = (own, swap(own, 1, 0), scale)
            kept.append(rest)
    moved = [swap(near[i], i % 2, 2 * (i // 2)) if i else near[i] for i in range(4)]
    arrived = [swap(close[i], i % 2, order[-1] + 2 * (i // 2)) for i in range(4)]
    layer_out, d_tokens = pl.pallas_call(
        functools.partial(finish_kernel, 4),
        out_shape=(shape(rows, features),) * 2,
        in_specs=[vmem] * 8,
        out_specs=(vmem,) * 2,
        cost_estimate=small,
        compiler_params=little,
        name="finish",
    )(moved[0], moved[2], arrived[0], arrived[2], moved[1], moved[3], arrived[1], arrived[3])

    groups = [[arrays[i] for arrays in kept] for i in range(2)]
    groups += [[arrays[i] for arrays in saved] for i in range(3)]
    operands = [array for group in groups for array in group]
    grad_shapes = [(1, part, units), (1, part, units), (1, units, part)]
    grad_gate, grad_up, grad_down = pl.pallas_call(
        functools.partial(grad_kernel, [len(group) for group in groups]),
        out_shape=tuple(shape(*dims) for dims in grad_shapes),
        in_specs=[vmem] * (len(operands) + len(last)),
        out_specs=(anywhere,) * 3,
        scratch_shapes=[pltpu.VMEM(dims, bf16) for dims in grad_shapes]
        + [pltpu.SemaphoreType.DMA((3,))],
        cost_estimate=busy,
        compiler_params=params,
        name="grads",
    )(*operands, *last)
    return (layer_out, d_tokens, grad_gate, grad_up, grad_down)


def slots(tokens, routes, gates, cotangent, w_gate, w_up, w_down):
    tok_rows, features = tokens.shape
    fanout = routes.shape[1]
    experts = lax.axis_size("expert")
    groups = lax.axis_size("dp")
    capacity = min(tok_rows, max(2, 2 * tok_rows * fanout // experts))
    assigned = tok_rows * fanout
    expert_ids = routes.reshape(assigned)
    onehot = (expert_ids[:, None] == jnp.arange(experts, dtype=jnp.int32)[None, :]).astype(
        jnp.float32
    )
    assign_iota = jnp.arange(assigned, dtype=jnp.int32)
    earlier = (assign_iota[:, None] > assign_iota[None, :]).astype(jnp.float32)
    prior_count = jnp.dot(earlier, onehot, precision=lax.Precision.HIGHEST)
    slot_index = jnp.sum(prior_count * onehot, axis=1).astype(jnp.int32)
    position = expert_ids * capacity + slot_index
    slot_map = (
        jnp.arange(experts * capacity, dtype=jnp.int32)[:, None] == position[None, :]
    ).astype(jnp.float32)
    token_owner = (
        assign_iota[:, None] // fanout == jnp.arange(tok_rows, dtype=jnp.int32)[None, :]
    ).astype(jnp.float32)
    dispatch = jnp.dot(slot_map, token_owner, precision=lax.Precision.HIGHEST)
    weighted = jnp.dot(
        slot_map, token_owner * gates.reshape(assigned)[:, None], precision=lax.Precision.HIGHEST
    )
    send_input = jnp.dot(
        dispatch.astype(jnp.bfloat16), tokens, preferred_element_type=jnp.float32
    ).astype(jnp.bfloat16)
    send_dout = jnp.dot(
        weighted, cotangent.astype(jnp.float32), precision=lax.Precision.HIGHEST
    ).astype(jnp.bfloat16)
    send_input = send_input.reshape(1, experts, capacity, features)
    send_dout = send_dout.reshape(1, experts, capacity, features)
    moved = (
        lax.all_to_all(send_input, "dp", split_axis=3, concat_axis=0, tiled=True),
        lax.all_to_all(send_dout, "dp", split_axis=3, concat_axis=0, tiled=True),
    )
    moved = (
        lax.all_to_all(moved[0], "expert", split_axis=1, concat_axis=1, tiled=True),
        lax.all_to_all(moved[1], "expert", split_axis=1, concat_axis=1, tiled=True),
    )
    part_width = moved[0].shape[3]
    total_rows = groups * experts * capacity
    input_rows = moved[0].reshape(total_rows, part_width)
    dout_rows = moved[1].reshape(total_rows, part_width)
    gate_local = w_gate[0]
    up_local = w_up[0]
    down_local = w_down[0]
    own_rows = total_rows // groups
    own_start = lax.axis_index("dp") * own_rows
    gate_part = jnp.dot(input_rows, gate_local, preferred_element_type=jnp.float32)
    up_part = jnp.dot(input_rows, up_local, preferred_element_type=jnp.float32)
    gate_all, up_all = (
        lax.psum(gate_part.astype(jnp.bfloat16), "dp").astype(jnp.float32),
        lax.psum(up_part.astype(jnp.bfloat16), "dp").astype(jnp.float32),
    )
    hidden = (jax.nn.silu(gate_all) * up_all).astype(jnp.bfloat16)
    gate_own = lax.dynamic_slice_in_dim(gate_all, own_start, own_rows, 0)
    up_own = lax.dynamic_slice_in_dim(up_all, own_start, own_rows, 0)
    out_slots = jnp.dot(hidden, down_local, preferred_element_type=jnp.float32).astype(jnp.bfloat16)
    grad_down = jnp.einsum(
        "rf,rd->fd", hidden, dout_rows, preferred_element_type=jnp.float32
    ).astype(jnp.bfloat16)
    dhidden_part = jnp.einsum(
        "rd,fd->rf", dout_rows, down_local, preferred_element_type=jnp.float32
    )
    dhidden_own = lax.psum_scatter(
        dhidden_part.astype(jnp.bfloat16), "dp", scatter_dimension=0, tiled=True
    ).astype(jnp.float32)
    sigmoid_gate = jax.nn.sigmoid(gate_own)
    silu_gate = gate_own * sigmoid_gate
    dgate_own = (
        dhidden_own * up_own * sigmoid_gate * (1.0 + gate_own * (1.0 - sigmoid_gate))
    ).astype(jnp.bfloat16)
    dup_own = (dhidden_own * silu_gate).astype(jnp.bfloat16)
    dgate_all, dup_all = (
        lax.all_gather(dgate_own, "dp", axis=0, tiled=True),
        lax.all_gather(dup_own, "dp", axis=0, tiled=True),
    )
    grad_gate = jnp.einsum(
        "rd,rf->df", input_rows, dgate_all, preferred_element_type=jnp.float32
    ).astype(jnp.bfloat16)
    grad_up = jnp.einsum(
        "rd,rf->df", input_rows, dup_all, preferred_element_type=jnp.float32
    ).astype(jnp.bfloat16)
    back_slots = (
        jnp.einsum("rf,df->rd", dgate_all, gate_local, preferred_element_type=jnp.float32)
        + jnp.einsum("rf,df->rd", dup_all, up_local, preferred_element_type=jnp.float32)
    ).astype(jnp.bfloat16)
    out_slots = out_slots.reshape(groups, experts, capacity, part_width)
    back_slots = back_slots.reshape(groups, experts, capacity, part_width)
    returned = (
        lax.all_to_all(out_slots, "expert", split_axis=1, concat_axis=1, tiled=True),
        lax.all_to_all(back_slots, "expert", split_axis=1, concat_axis=1, tiled=True),
    )
    returned = (
        lax.all_to_all(returned[0], "dp", split_axis=0, concat_axis=3, tiled=True),
        lax.all_to_all(returned[1], "dp", split_axis=0, concat_axis=3, tiled=True),
    )
    out_tokens = returned[0].reshape(experts * capacity, features)
    back_tokens = returned[1].reshape(experts * capacity, features)
    layer_out = jnp.dot(
        weighted.T, out_tokens.astype(jnp.float32), precision=lax.Precision.HIGHEST
    ).astype(jnp.bfloat16)
    d_tokens = jnp.dot(
        dispatch.T.astype(jnp.bfloat16), back_tokens, preferred_element_type=jnp.float32
    ).astype(jnp.bfloat16)
    return (layer_out, d_tokens, grad_gate[None], grad_up[None], grad_down[None])


def local(tokens, routes, gates, cotangent, w_gate, w_up, w_down):
    rows, fanout = routes.shape
    experts, groups = lax.axis_size("expert"), lax.axis_size("dp")
    capacity = min(rows, max(2, 2 * rows * fanout // experts))
    bits = experts & (experts - 1) == 0 and experts % 4 == 0
    form = dense if capacity == rows and groups == 2 and bits else slots
    return form(tokens, routes, gates, cotangent, w_gate, w_up, w_down)


def solution(mesh):
    return jax.shard_map(
        local,
        mesh=mesh,
        in_specs=(
            P(("dp", "expert"), None),
            P(("dp", "expert"), None),
            P(("dp", "expert"), None),
            P(("dp", "expert"), None),
            P("expert", "dp", None),
            P("expert", "dp", None),
            P("expert", None, "dp"),
        ),
        out_specs=(
            P(("dp", "expert"), None),
            P(("dp", "expert"), None),
            P("expert", "dp", None),
            P("expert", "dp", None),
            P("expert", None, "dp"),
        ),
        check_vma=False,
    )
```

```python
import functools

import jax
import jax.numpy as jnp
from jax import lax
from jax.experimental import pallas as pl
from jax.experimental.pallas import tpu as pltpu
from jax.sharding import PartitionSpec as P


def swap(value, dp_bit, expert_bits):
    groups, experts = lax.axis_size("dp"), lax.axis_size("expert")
    if dp_bit == 0:
        pairs = [(e, e ^ expert_bits) for e in range(experts)]
        return lax.ppermute(value, "expert", pairs)
    pairs = [
        (d * experts + e, (d ^ dp_bit) * experts + (e ^ expert_bits))
        for d in range(groups)
        for e in range(experts)
    ]
    return lax.ppermute(value, ("dp", "expert"), pairs)


def prepare_kernel(tokens_ref, routes_ref, gates_ref, cotangent_ref, mine_ref, other_ref, *, experts, part):
    rows, fanout = tokens_ref.shape[0], routes_ref.shape[0]
    width = mine_ref.shape[1] - 2 * part
    routes, gates = routes_ref[...].T, gates_ref[...].T
    lane = lax.broadcasted_iota(jnp.int32, (rows, width), 1)
    named = lax.rem(lane, experts)
    table = jnp.zeros((rows, width), jnp.float32)
    for k in range(fanout):
        table = table + jnp.where(routes[:, k : k + 1] == named, gates[:, k : k + 1], 0.0)
    high = table.astype(jnp.bfloat16).astype(jnp.float32)
    middle = (table - high).astype(jnp.bfloat16).astype(jnp.float32)
    low = table - high - middle
    piece = lane // experts
    extra = jnp.where(piece == 0, high, jnp.where(piece == 1, middle, jnp.where(piece == 2, low, 0.0)))
    extra = extra.astype(jnp.bfloat16)
    dp_index = lax.axis_index("dp")
    for ref, owner in ((mine_ref, dp_index), (other_ref, 1 - dp_index)):
        columns = pl.ds(pl.multiple_of(owner * part, part), part)
        ref[:, :part] = tokens_ref[:, columns]
        ref[:, part : 2 * part] = cotangent_ref[:, columns]
        ref[:, 2 * part :] = extra


def begin(copies):
    for copy in copies:
        copy.start()
    return copies


def partial_kernel(count, parts, experts, part, *refs):
    f32, bf16 = jnp.float32, jnp.bfloat16
    pieces, weights = refs[:count], refs[count : count + 3]
    scale_ref, input_ref, dout_ref = refs[-3:]
    own_refs = refs[-3 - parts : -3]
    gate_ref, up_ref, down_ref = (weight.at[0] for weight in weights)
    units = gate_ref.shape[1]
    start = 0
    for piece in pieces:
        rows = piece.shape[0]
        here = slice(start, start + rows)
        start += rows
        extra = piece[:, 2 * part :].astype(f32)
        lane = lax.broadcasted_iota(jnp.int32, extra.shape, 1)
        scale = jnp.sum(
            jnp.where(lax.rem(lane, experts) == lax.axis_index("expert"), extra, 0.0), axis=1, keepdims=True
        )
        scale_ref[here, :] = jnp.broadcast_to(scale, (rows, scale_ref.shape[1]))
        input_ref[here, :] = piece[:, :part]
        dout_ref[here, :] = (scale * piece[:, part : 2 * part].astype(f32)).astype(bf16)
    def store(columns, value):
        start = 0
        for ref in own_refs:
            ref[:, columns] = value[start : start + ref.shape[0]].astype(bf16)
            start += ref.shape[0]

    for i, weight in enumerate((gate_ref, up_ref)):
        store(
            slice(i * units, (i + 1) * units),
            jnp.dot(input_ref[...], weight[...], preferred_element_type=f32),
        )
    across = (((1,), (1,)), ((), ()))
    store(
        slice(2 * units, 3 * units),
        lax.dot_general(dout_ref[...], down_ref[...], across, preferred_element_type=f32),
    )


def expert_kernel(block, skipped, parts, first, own_ref, their_ref, scale_ref, *refs):
    f32, bf16 = jnp.float32, jnp.bfloat16
    weights, refs = refs[:3], refs[3 + skipped :]
    pieces, refs = refs[:parts], refs[parts:]
    hidden_ref, dgate_ref, dup_ref = refs
    gate_ref, up_ref, down_ref = (weight.at[0] for weight in weights)
    rows = own_ref.shape[0]
    part, units = gate_ref.shape
    blocks = [their_ref[(i ^ 1) * block : ((i ^ 1) + 1) * block, :] for i in range(rows // block)]
    total = own_ref[...].astype(f32) + jnp.concatenate(blocks, axis=0).astype(f32)
    gate, up, dhidden = total[:, :units], total[:, units : 2 * units], total[:, 2 * units :]
    sigmoid = jax.nn.sigmoid(gate)
    silu = gate * sigmoid
    hidden_ref[...] = (silu * up).astype(bf16)
    dgate_ref[...] = (dhidden * up * sigmoid * (1.0 + gate * (1.0 - sigmoid))).astype(bf16)
    dup_ref[...] = (dhidden * silu).astype(bf16)
    half = rows // parts
    out = scale_ref[first : first + rows, :1] * jnp.dot(hidden_ref[...], down_ref[...], preferred_element_type=f32)
    for i, ref in enumerate(pieces):
        ref[:, :part] = out[i * half : (i + 1) * half].astype(bf16)
    across = (((1,), (1,)), ((), ()))
    back = lax.dot_general(dgate_ref[...], gate_ref[...], across, preferred_element_type=f32)
    back = back + lax.dot_general(dup_ref[...], up_ref[...], across, preferred_element_type=f32)
    for i, ref in enumerate(pieces):
        ref[:, part:] = back[i * half : (i + 1) * half].astype(bf16)


def merge_kernel(counts, parts, *refs):
    terms, first = [], 0
    for count in counts:
        group = refs[first : first + count]
        terms.append(jnp.concatenate([ref[...].astype(jnp.float32) for ref in group], axis=0))
        first += count
    total = sum(terms)
    start = 0
    for piece in refs[-parts:]:
        rows = piece.shape[0]
        piece[...] = total[start : start + rows].astype(piece.dtype)
        start += rows


def gather_kernel(count, parts, *refs):
    rows = jnp.concatenate([ref[...] for ref in refs[:count]], axis=0)
    start = 0
    for piece in refs[-parts:]:
        piece[...] = rows[start : start + piece.shape[0]]
        start += piece.shape[0]


def finish_kernel(count, *refs):
    f32 = jnp.float32
    out_ref, back_ref = refs[2 * count :]
    part = refs[0].shape[1] // 2
    dp_index = lax.axis_index("dp")
    for owner, terms in ((dp_index, refs[:count]), (1 - dp_index, refs[count : 2 * count])):
        columns = pl.ds(pl.multiple_of(owner * part, part), part)
        for ref, start in ((out_ref, 0), (back_ref, part)):
            total = sum(term[:, start : start + part].astype(f32) for term in terms)
            ref[:, columns] = total.astype(ref.dtype)


def grad_kernel(counts, *refs):
    bf16 = jnp.bfloat16
    groups, start = [], 0
    for count in counts:
        groups.append(refs[start : start + count])
        start += count
    outs, token_ref, results, done = refs[-8:-5], refs[-5], refs[-4:-1], refs[-1]
    token_ref[...] = jnp.zeros_like(token_ref)

    def rows_of(group):
        return jnp.concatenate([ref[...] for ref in group], axis=0)

    over_rows = (((0,), (0,)), ((), ()))
    copies = []
    for i, (left, right) in enumerate(((0, 3), (0, 4), (2, 1))):
        results[i][0] = lax.dot_general(
            rows_of(groups[left]),
            rows_of(groups[right]),
            over_rows,
            preferred_element_type=jnp.float32,
        ).astype(bf16)
        copies += begin([pltpu.make_async_copy(results[i], outs[i], done.at[i])])
    for copy in copies:
        copy.wait()


def dense(tokens, routes, gates, cotangent, w_gate, w_up, w_down):
    f32, bf16 = jnp.float32, jnp.bfloat16
    rows, features = tokens.shape
    experts = lax.axis_size("expert")
    part, units = w_gate.shape[1:]
    wide = 2 * part + -(-3 * experts // 128) * 128
    params = pltpu.CompilerParams(vmem_limit_bytes=20 * 1024 * 1024)
    little = pltpu.CompilerParams(vmem_limit_bytes=4 * 1024 * 1024)
    long = pl.CostEstimate(flops=int(1e10), bytes_accessed=1000, transcendentals=0)
    small = pl.CostEstimate(flops=1000, bytes_accessed=1000, transcendentals=0)
    vmem = pl.BlockSpec(memory_space=pltpu.VMEM)
    anywhere = pl.BlockSpec(memory_space=pl.ANY)

    def shape(*dims, dtype=bf16):
        return jax.ShapeDtypeStruct(dims, dtype)

    mine, other = pl.pallas_call(
        functools.partial(prepare_kernel, experts=experts, part=part),
        out_shape=(shape(rows, wide), shape(rows, wide)),
        in_specs=[vmem] * 4,
        out_specs=(vmem, vmem),
        cost_estimate=long,
        compiler_params=pltpu.CompilerParams(vmem_limit_bytes=58 * 1024 * 1024),
        name="prepare",
    )(tokens, routes.T, gates.T, cotangent)

    weights = (w_gate, w_up, w_down)
    last, kept = [], []

    def partials(pieces, sizes):
        nonlocal last
        count = sum(piece.shape[0] for piece in pieces)
        outs = pl.pallas_call(
            functools.partial(partial_kernel, len(pieces), len(sizes), experts, part),
            out_shape=tuple(shape(size, 3 * units) for size in sizes)
            + (shape(count, 128, dtype=f32), shape(count, part), shape(count, part)),
            in_specs=[vmem] * len(pieces) + [vmem] * (3 + len(last)),
            out_specs=(vmem,) * (len(sizes) + 3),
            cost_estimate=small,
            compiler_params=params,
            name="partials",
        )(*pieces, *weights, *last)
        last = [outs[len(sizes)]]
        return outs[: len(sizes)], outs[-3:]

    def expert(own, theirs, scale, first, parts):
        nonlocal last
        count = own.shape[0]
        outs = pl.pallas_call(
            functools.partial(expert_kernel, rows, len(last), parts, first),
            out_shape=(shape(count // parts, 2 * part),) * parts + (shape(count, units),) * 3,
            in_specs=[vmem] * 3 + [vmem] * (3 + len(last)),
            out_specs=(vmem,) * (parts + 3),
            cost_estimate=small,
            compiler_params=params,
            name="expert",
        )(own, theirs, scale, *weights, *last)
        last = [outs[0]]
        return outs[:parts], outs[parts:]

    def merge(terms, sizes):
        nonlocal last
        pieces = [piece for term in terms for piece in term]
        outs = pl.pallas_call(
            functools.partial(merge_kernel, [len(term) for term in terms], len(sizes)),
            out_shape=tuple(shape(size, pieces[0].shape[1]) for size in sizes),
            in_specs=[vmem] * (len(pieces) + len(last)),
            out_specs=(vmem,) * len(sizes),
            cost_estimate=small,
            compiler_params=little,
            name="merge",
        )(*pieces, *last)
        last = [outs[0]]
        return list(outs)

    def gather(pieces, sizes):
        nonlocal last
        outs = pl.pallas_call(
            functools.partial(gather_kernel, len(pieces), len(sizes)),
            out_shape=tuple(shape(size, pieces[0].shape[1]) for size in sizes),
            in_specs=[vmem] * (len(pieces) + len(last)),
            out_specs=(vmem,) * len(sizes),
            cost_estimate=small if last else long,
            compiler_params=little,
            name="gather",
        )(*pieces, *last)
        last = [outs[0]]
        return list(outs)

    planes = experts // 4
    far = list(range(planes - 1, 1, -1))
    half = 2 * rows
    [quad] = gather([mine, swap(other, 1, 0), swap(mine, 0, 2), swap(other, 1, 2)], [2 * half])
    quads = [quad] + [swap(quad, 0, 4 * z) for z in range(1, planes)]
    order, sent, saved, keeps, received, arrivals, total = [], {}, {}, {}, {}, {}, []

    def project(z, side):
        piece = swap(quads[z], 0, 1) if side else quads[z]
        [own], (scale, *rest) = partials([piece], [piece.shape[0]])
        sent[z, side] = (own, swap(own, 1, 0), scale)
        kept.append(rest)
        order.append((z, side))

    def act(z, side):
        [piece], saved[z, side] = expert(*sent[z, side], 0, 1)
        if side:
            received[z] = swap(piece, 0, 1)
        else:
            keeps[z] = piece

    def send_sum(z):
        [piece] = merge([[keeps[z]], [received[z]]], [2 * half])
        arrivals[z] = swap(piece, 0, 4 * z)

    def collect(z):
        total[:] = merge([[piece] for piece in total] + [[arrivals.pop(z)]], [2 * half])

    def run_grads():
        nonlocal last
        groups = [[arrays[i] for arrays in kept] for i in range(2)]
        groups += [[saved[key][i] for key in order] for i in range(3)]
        operands = [array for group in groups for array in group]
        grad_shapes = [(1, part, units), (1, part, units), (1, units, part)]
        grads = pl.pallas_call(
            functools.partial(grad_kernel, [len(group) for group in groups]),
            out_shape=tuple(shape(*dims) for dims in grad_shapes) + (shape(8, 128, dtype=f32),),
            in_specs=[vmem] * (len(operands) + len(last)),
            out_specs=(anywhere,) * 3 + (vmem,),
            scratch_shapes=[pltpu.VMEM(dims, bf16) for dims in grad_shapes]
            + [pltpu.SemaphoreType.DMA((3,))],
            cost_estimate=small,
            compiler_params=params,
            name="grads",
        )(*operands, *last)
        last = [grads[3]]
        return grads[:3]

    project(0, 0)
    project(1, 0)
    if far:
        project(far[0], 0)
    act(0, 0)
    act(1, 0)
    if far:
        project(far[0], 1)
    for i, z in enumerate(far):
        final = i + 1 == len(far)
        project(1 if final else far[i + 1], 1 if final else 0)
        act(z, 0)
        act(z, 1)
        project(0 if final else far[i + 1], 1)
        if i > 0:
            collect(far[i - 1])
        send_sum(z)
    if not far:
        project(1, 1)
        project(0, 1)
    act(1, 1)
    send_sum(1)
    act(0, 1)
    grad_gate, grad_up, grad_down = run_grads()
    for z in [*far[-1:], 1]:
        collect(z)
    pieces = merge(
        [[piece] for piece in (*total, keeps[0], received[0])], [rows] * 4
    )
    moved = [swap(pieces[i], i % 2, 2 * (i // 2)) if i else pieces[i] for i in range(4)]
    layer_out, d_tokens = pl.pallas_call(
        functools.partial(finish_kernel, 2),
        out_shape=(shape(rows, features),) * 2,
        in_specs=[vmem] * 4,
        out_specs=(vmem,) * 2,
        cost_estimate=small,
        compiler_params=little,
        name="finish",
    )(moved[0], moved[2], moved[1], moved[3])

    return (layer_out, d_tokens, grad_gate, grad_up, grad_down)


def slots(tokens, routes, gates, cotangent, w_gate, w_up, w_down):
    tok_rows, features = tokens.shape
    fanout = routes.shape[1]
    experts = lax.axis_size("expert")
    groups = lax.axis_size("dp")
    capacity = min(tok_rows, max(2, 2 * tok_rows * fanout // experts))
    assigned = tok_rows * fanout
    expert_ids = routes.reshape(assigned)
    onehot = (expert_ids[:, None] == jnp.arange(experts, dtype=jnp.int32)[None, :]).astype(
        jnp.float32
    )
    assign_iota = jnp.arange(assigned, dtype=jnp.int32)
    earlier = (assign_iota[:, None] > assign_iota[None, :]).astype(jnp.float32)
    prior_count = jnp.dot(earlier, onehot, precision=lax.Precision.HIGHEST)
    slot_index = jnp.sum(prior_count * onehot, axis=1).astype(jnp.int32)
    position = expert_ids * capacity + slot_index
    slot_map = (
        jnp.arange(experts * capacity, dtype=jnp.int32)[:, None] == position[None, :]
    ).astype(jnp.float32)
    token_owner = (
        assign_iota[:, None] // fanout == jnp.arange(tok_rows, dtype=jnp.int32)[None, :]
    ).astype(jnp.float32)
    dispatch = jnp.dot(slot_map, token_owner, precision=lax.Precision.HIGHEST)
    weighted = jnp.dot(
        slot_map, token_owner * gates.reshape(assigned)[:, None], precision=lax.Precision.HIGHEST
    )
    send_input = jnp.dot(
        dispatch.astype(jnp.bfloat16), tokens, preferred_element_type=jnp.float32
    ).astype(jnp.bfloat16)
    send_dout = jnp.dot(
        weighted, cotangent.astype(jnp.float32), precision=lax.Precision.HIGHEST
    ).astype(jnp.bfloat16)
    send_input = send_input.reshape(1, experts, capacity, features)
    send_dout = send_dout.reshape(1, experts, capacity, features)
    moved = (
        lax.all_to_all(send_input, "dp", split_axis=3, concat_axis=0, tiled=True),
        lax.all_to_all(send_dout, "dp", split_axis=3, concat_axis=0, tiled=True),
    )
    moved = (
        lax.all_to_all(moved[0], "expert", split_axis=1, concat_axis=1, tiled=True),
        lax.all_to_all(moved[1], "expert", split_axis=1, concat_axis=1, tiled=True),
    )
    part_width = moved[0].shape[3]
    total_rows = groups * experts * capacity
    input_rows = moved[0].reshape(total_rows, part_width)
    dout_rows = moved[1].reshape(total_rows, part_width)
    gate_local = w_gate[0]
    up_local = w_up[0]
    down_local = w_down[0]
    own_rows = total_rows // groups
    own_start = lax.axis_index("dp") * own_rows
    gate_part = jnp.dot(input_rows, gate_local, preferred_element_type=jnp.float32)
    up_part = jnp.dot(input_rows, up_local, preferred_element_type=jnp.float32)
    gate_all, up_all = (
        lax.psum(gate_part.astype(jnp.bfloat16), "dp").astype(jnp.float32),
        lax.psum(up_part.astype(jnp.bfloat16), "dp").astype(jnp.float32),
    )
    hidden = (jax.nn.silu(gate_all) * up_all).astype(jnp.bfloat16)
    gate_own = lax.dynamic_slice_in_dim(gate_all, own_start, own_rows, 0)
    up_own = lax.dynamic_slice_in_dim(up_all, own_start, own_rows, 0)
    out_slots = jnp.dot(hidden, down_local, preferred_element_type=jnp.float32).astype(jnp.bfloat16)
    grad_down = jnp.einsum(
        "rf,rd->fd", hidden, dout_rows, preferred_element_type=jnp.float32
    ).astype(jnp.bfloat16)
    dhidden_part = jnp.einsum(
        "rd,fd->rf", dout_rows, down_local, preferred_element_type=jnp.float32
    )
    dhidden_own = lax.psum_scatter(
        dhidden_part.astype(jnp.bfloat16), "dp", scatter_dimension=0, tiled=True
    ).astype(jnp.float32)
    sigmoid_gate = jax.nn.sigmoid(gate_own)
    silu_gate = gate_own * sigmoid_gate
    dgate_own = (
        dhidden_own * up_own * sigmoid_gate * (1.0 + gate_own * (1.0 - sigmoid_gate))
    ).astype(jnp.bfloat16)
    dup_own = (dhidden_own * silu_gate).astype(jnp.bfloat16)
    dgate_all, dup_all = (
        lax.all_gather(dgate_own, "dp", axis=0, tiled=True),
        lax.all_gather(dup_own, "dp", axis=0, tiled=True),
    )
    grad_gate = jnp.einsum(
        "rd,rf->df", input_rows, dgate_all, preferred_element_type=jnp.float32
    ).astype(jnp.bfloat16)
    grad_up = jnp.einsum(
        "rd,rf->df", input_rows, dup_all, preferred_element_type=jnp.float32
    ).astype(jnp.bfloat16)
    back_slots = (
        jnp.einsum("rf,df->rd", dgate_all, gate_local, preferred_element_type=jnp.float32)
        + jnp.einsum("rf,df->rd", dup_all, up_local, preferred_element_type=jnp.float32)
    ).astype(jnp.bfloat16)
    out_slots = out_slots.reshape(groups, experts, capacity, part_width)
    back_slots = back_slots.reshape(groups, experts, capacity, part_width)
    returned = (
        lax.all_to_all(out_slots, "expert", split_axis=1, concat_axis=1, tiled=True),
        lax.all_to_all(back_slots, "expert", split_axis=1, concat_axis=1, tiled=True),
    )
    returned = (
        lax.all_to_all(returned[0], "dp", split_axis=0, concat_axis=3, tiled=True),
        lax.all_to_all(returned[1], "dp", split_axis=0, concat_axis=3, tiled=True),
    )
    out_tokens = returned[0].reshape(experts * capacity, features)
    back_tokens = returned[1].reshape(experts * capacity, features)
    layer_out = jnp.dot(
        weighted.T, out_tokens.astype(jnp.float32), precision=lax.Precision.HIGHEST
    ).astype(jnp.bfloat16)
    d_tokens = jnp.dot(
        dispatch.T.astype(jnp.bfloat16), back_tokens, preferred_element_type=jnp.float32
    ).astype(jnp.bfloat16)
    return (layer_out, d_tokens, grad_gate[None], grad_up[None], grad_down[None])


def local(tokens, routes, gates, cotangent, w_gate, w_up, w_down):
    rows, fanout = routes.shape
    experts, groups = lax.axis_size("expert"), lax.axis_size("dp")
    capacity = min(rows, max(2, 2 * rows * fanout // experts))
    bits = experts & (experts - 1) == 0 and experts >= 8
    form = dense if capacity == rows and groups == 2 and bits else slots
    return form(tokens, routes, gates, cotangent, w_gate, w_up, w_down)


def solution(mesh):
    return jax.shard_map(
        local,
        mesh=mesh,
        in_specs=(
            P(("dp", "expert"), None),
            P(("dp", "expert"), None),
            P(("dp", "expert"), None),
            P(("dp", "expert"), None),
            P("expert", "dp", None),
            P("expert", "dp", None),
            P("expert", None, "dp"),
        ),
        out_specs=(
            P(("dp", "expert"), None),
            P(("dp", "expert"), None),
            P("expert", "dp", None),
            P("expert", "dp", None),
            P("expert", None, "dp"),
        ),
        check_vma=False,
    )
```

```python
import functools

import jax
import jax.numpy as jnp
from jax import lax
from jax.experimental import pallas as pl
from jax.experimental.pallas import tpu as pltpu
from jax.sharding import PartitionSpec as P


def swap(value, dp_bit, expert_bits):
    groups, experts = lax.axis_size("dp"), lax.axis_size("expert")
    if dp_bit == 0:
        pairs = [(e, e ^ expert_bits) for e in range(experts)]
        return lax.ppermute(value, "expert", pairs)
    pairs = [
        (d * experts + e, (d ^ dp_bit) * experts + (e ^ expert_bits))
        for d in range(groups)
        for e in range(experts)
    ]
    return lax.ppermute(value, ("dp", "expert"), pairs)


def prepare_kernel(tokens_ref, routes_ref, gates_ref, cotangent_ref, mine_ref, other_ref, *, experts, part):
    rows, fanout = tokens_ref.shape[0], routes_ref.shape[0]
    width = mine_ref.shape[1] - 2 * part
    routes, gates = routes_ref[...].T, gates_ref[...].T
    lane = lax.broadcasted_iota(jnp.int32, (rows, width), 1)
    named = lax.rem(lane, experts)
    table = jnp.zeros((rows, width), jnp.float32)
    for k in range(fanout):
        table = table + jnp.where(routes[:, k : k + 1] == named, gates[:, k : k + 1], 0.0)
    high = table.astype(jnp.bfloat16).astype(jnp.float32)
    middle = (table - high).astype(jnp.bfloat16).astype(jnp.float32)
    low = table - high - middle
    piece = lane // experts
    extra = jnp.where(piece == 0, high, jnp.where(piece == 1, middle, jnp.where(piece == 2, low, 0.0)))
    extra = extra.astype(jnp.bfloat16)
    dp_index = lax.axis_index("dp")
    for ref, owner in ((mine_ref, dp_index), (other_ref, 1 - dp_index)):
        columns = pl.ds(pl.multiple_of(owner * part, part), part)
        ref[:, :part] = tokens_ref[:, columns]
        ref[:, part : 2 * part] = cotangent_ref[:, columns]
        ref[:, 2 * part :] = extra


def begin(copies):
    for copy in copies:
        copy.start()
    return copies


def partial_kernel(count, parts, experts, part, *refs):
    f32, bf16 = jnp.float32, jnp.bfloat16
    pieces, weights = refs[:count], refs[count : count + 3]
    scale_ref, input_ref, dout_ref = refs[-3:]
    own_refs = refs[-3 - parts : -3]
    gate_ref, up_ref, down_ref = (weight.at[0] for weight in weights)
    units = gate_ref.shape[1]
    start = 0
    for piece in pieces:
        rows = piece.shape[0]
        here = slice(start, start + rows)
        start += rows
        extra = piece[:, 2 * part :].astype(f32)
        lane = lax.broadcasted_iota(jnp.int32, extra.shape, 1)
        scale = jnp.sum(
            jnp.where(lax.rem(lane, experts) == lax.axis_index("expert"), extra, 0.0), axis=1, keepdims=True
        )
        scale_ref[here, :] = jnp.broadcast_to(scale, (rows, scale_ref.shape[1]))
        input_ref[here, :] = piece[:, :part]
        dout_ref[here, :] = (scale * piece[:, part : 2 * part].astype(f32)).astype(bf16)
    def store(columns, value):
        start = 0
        for ref in own_refs:
            ref[:, columns] = value[start : start + ref.shape[0]].astype(bf16)
            start += ref.shape[0]

    for i, weight in enumerate((gate_ref, up_ref)):
        store(
            slice(i * units, (i + 1) * units),
            jnp.dot(input_ref[...], weight[...], preferred_element_type=f32),
        )
    across = (((1,), (1,)), ((), ()))
    store(
        slice(2 * units, 3 * units),
        lax.dot_general(dout_ref[...], down_ref[...], across, preferred_element_type=f32),
    )


def expert_kernel(block, skipped, parts, first, own_ref, their_ref, scale_ref, *refs):
    f32, bf16 = jnp.float32, jnp.bfloat16
    weights, refs = refs[:3], refs[3 + skipped :]
    pieces, refs = refs[:parts], refs[parts:]
    hidden_ref, dgate_ref, dup_ref = refs
    gate_ref, up_ref, down_ref = (weight.at[0] for weight in weights)
    rows = own_ref.shape[0]
    part, units = gate_ref.shape
    blocks = [their_ref[(i ^ 1) * block : ((i ^ 1) + 1) * block, :] for i in range(rows // block)]
    total = own_ref[...].astype(f32) + jnp.concatenate(blocks, axis=0).astype(f32)
    gate, up, dhidden = total[:, :units], total[:, units : 2 * units], total[:, 2 * units :]
    sigmoid = jax.nn.sigmoid(gate)
    silu = gate * sigmoid
    hidden_ref[...] = (silu * up).astype(bf16)
    dgate_ref[...] = (dhidden * up * sigmoid * (1.0 + gate * (1.0 - sigmoid))).astype(bf16)
    dup_ref[...] = (dhidden * silu).astype(bf16)
    half = rows // parts
    out = scale_ref[first : first + rows, :1] * jnp.dot(hidden_ref[...], down_ref[...], preferred_element_type=f32)
    for i, ref in enumerate(pieces):
        ref[:, :part] = out[i * half : (i + 1) * half].astype(bf16)
    across = (((1,), (1,)), ((), ()))
    back = lax.dot_general(dgate_ref[...], gate_ref[...], across, preferred_element_type=f32)
    back = back + lax.dot_general(dup_ref[...], up_ref[...], across, preferred_element_type=f32)
    for i, ref in enumerate(pieces):
        ref[:, part:] = back[i * half : (i + 1) * half].astype(bf16)


def merge_kernel(counts, parts, *refs):
    terms, first = [], 0
    for count in counts:
        group = refs[first : first + count]
        terms.append(jnp.concatenate([ref[...].astype(jnp.float32) for ref in group], axis=0))
        first += count
    total = sum(terms)
    start = 0
    for piece in refs[-parts:]:
        rows = piece.shape[0]
        piece[...] = total[start : start + rows].astype(piece.dtype)
        start += rows


def gather_kernel(count, parts, *refs):
    rows = jnp.concatenate([ref[...] for ref in refs[:count]], axis=0)
    start = 0
    for piece in refs[-parts:]:
        piece[...] = rows[start : start + piece.shape[0]]
        start += piece.shape[0]


def finish_kernel(count, *refs):
    f32 = jnp.float32
    out_ref, back_ref = refs[2 * count :]
    part = refs[0].shape[1] // 2
    dp_index = lax.axis_index("dp")
    for owner, terms in ((dp_index, refs[:count]), (1 - dp_index, refs[count : 2 * count])):
        columns = pl.ds(pl.multiple_of(owner * part, part), part)
        for ref, start in ((out_ref, 0), (back_ref, part)):
            total = sum(term[:, start : start + part].astype(f32) for term in terms)
            ref[:, columns] = total.astype(ref.dtype)


def grad_kernel(counts, *refs):
    bf16 = jnp.bfloat16
    groups, start = [], 0
    for count in counts:
        groups.append(refs[start : start + count])
        start += count
    outs, token_ref, results, done = refs[-8:-5], refs[-5], refs[-4:-1], refs[-1]
    token_ref[...] = jnp.zeros_like(token_ref)

    def rows_of(group):
        return jnp.concatenate([ref[...] for ref in group], axis=0)

    over_rows = (((0,), (0,)), ((), ()))
    copies = []
    for i, (left, right) in enumerate(((0, 3), (0, 4), (2, 1))):
        results[i][0] = lax.dot_general(
            rows_of(groups[left]),
            rows_of(groups[right]),
            over_rows,
            preferred_element_type=jnp.float32,
        ).astype(bf16)
        copies += begin([pltpu.make_async_copy(results[i], outs[i], done.at[i])])
    for copy in copies:
        copy.wait()


def dense(tokens, routes, gates, cotangent, w_gate, w_up, w_down):
    f32, bf16 = jnp.float32, jnp.bfloat16
    rows, features = tokens.shape
    experts = lax.axis_size("expert")
    part, units = w_gate.shape[1:]
    wide = 2 * part + -(-3 * experts // 128) * 128
    params = pltpu.CompilerParams(vmem_limit_bytes=20 * 1024 * 1024)
    little = pltpu.CompilerParams(vmem_limit_bytes=4 * 1024 * 1024)
    long = pl.CostEstimate(flops=int(1e10), bytes_accessed=1000, transcendentals=0)
    small = pl.CostEstimate(flops=1000, bytes_accessed=1000, transcendentals=0)
    vmem = pl.BlockSpec(memory_space=pltpu.VMEM)
    anywhere = pl.BlockSpec(memory_space=pl.ANY)

    def shape(*dims, dtype=bf16):
        return jax.ShapeDtypeStruct(dims, dtype)

    mine, other = pl.pallas_call(
        functools.partial(prepare_kernel, experts=experts, part=part),
        out_shape=(shape(rows, wide), shape(rows, wide)),
        in_specs=[vmem] * 4,
        out_specs=(vmem, vmem),
        cost_estimate=long,
        compiler_params=pltpu.CompilerParams(vmem_limit_bytes=58 * 1024 * 1024),
        name="prepare",
    )(tokens, routes.T, gates.T, cotangent)

    weights = (w_gate, w_up, w_down)
    last, kept = [], []

    def partials(pieces, sizes):
        nonlocal last
        count = sum(piece.shape[0] for piece in pieces)
        outs = pl.pallas_call(
            functools.partial(partial_kernel, len(pieces), len(sizes), experts, part),
            out_shape=tuple(shape(size, 3 * units) for size in sizes)
            + (shape(count, 128, dtype=f32), shape(count, part), shape(count, part)),
            in_specs=[vmem] * len(pieces) + [vmem] * (3 + len(last)),
            out_specs=(vmem,) * (len(sizes) + 3),
            cost_estimate=small,
            compiler_params=params,
            name="partials",
        )(*pieces, *weights, *last)
        last = [outs[len(sizes)]]
        return outs[: len(sizes)], outs[-3:]

    def expert(own, theirs, scale, first, parts):
        nonlocal last
        count = own.shape[0]
        outs = pl.pallas_call(
            functools.partial(expert_kernel, rows, len(last), parts, first),
            out_shape=(shape(count // parts, 2 * part),) * parts + (shape(count, units),) * 3,
            in_specs=[vmem] * 3 + [vmem] * (3 + len(last)),
            out_specs=(vmem,) * (parts + 3),
            cost_estimate=small,
            compiler_params=params,
            name="expert",
        )(own, theirs, scale, *weights, *last)
        last = [outs[0]]
        return outs[:parts], outs[parts:]

    def merge(terms, sizes):
        nonlocal last
        pieces = [piece for term in terms for piece in term]
        outs = pl.pallas_call(
            functools.partial(merge_kernel, [len(term) for term in terms], len(sizes)),
            out_shape=tuple(shape(size, pieces[0].shape[1]) for size in sizes),
            in_specs=[vmem] * (len(pieces) + len(last)),
            out_specs=(vmem,) * len(sizes),
            cost_estimate=small,
            compiler_params=little,
            name="merge",
        )(*pieces, *last)
        last = [outs[0]]
        return list(outs)

    def gather(pieces, sizes):
        nonlocal last
        outs = pl.pallas_call(
            functools.partial(gather_kernel, len(pieces), len(sizes)),
            out_shape=tuple(shape(size, pieces[0].shape[1]) for size in sizes),
            in_specs=[vmem] * (len(pieces) + len(last)),
            out_specs=(vmem,) * len(sizes),
            cost_estimate=small if last else long,
            compiler_params=little,
            name="gather",
        )(*pieces, *last)
        last = [outs[0]]
        return list(outs)

    planes = experts // 4
    far = list(range(planes - 1, 1, -1))
    half = 2 * rows
    [quad] = gather([mine, swap(other, 1, 0), swap(mine, 0, 2), swap(other, 1, 2)], [2 * half])
    quads = [quad] + [swap(quad, 0, 4 * z) for z in range(1, planes)]
    order, sent, saved, keeps, received, arrivals, total = [], {}, {}, {}, {}, {}, []

    def project(z, side):
        piece = swap(quads[z], 0, 1) if side else quads[z]
        [own], (scale, *rest) = partials([piece], [piece.shape[0]])
        sent[z, side] = (own, swap(own, 1, 0), scale)
        kept.append(rest)
        order.append((z, side))

    def act(z, side):
        [piece], saved[z, side] = expert(*sent[z, side], 0, 1)
        if side:
            received[z] = swap(piece, 0, 1)
        else:
            keeps[z] = piece

    def send_sum(z):
        [piece] = merge([[keeps[z]], [received[z]]], [2 * half])
        arrivals[z] = swap(piece, 0, 4 * z)

    def collect(z):
        total[:] = merge([[piece] for piece in total] + [[arrivals.pop(z)]], [2 * half])

    def run_grads():
        nonlocal last
        groups = [[arrays[i] for arrays in kept] for i in range(2)]
        groups += [[saved[key][i] for key in order] for i in range(3)]
        operands = [array for group in groups for array in group]
        grad_shapes = [(1, part, units), (1, part, units), (1, units, part)]
        grads = pl.pallas_call(
            functools.partial(grad_kernel, [len(group) for group in groups]),
            out_shape=tuple(shape(*dims) for dims in grad_shapes) + (shape(8, 128, dtype=f32),),
            in_specs=[vmem] * (len(operands) + len(last)),
            out_specs=(anywhere,) * 3 + (vmem,),
            scratch_shapes=[pltpu.VMEM(dims, bf16) for dims in grad_shapes]
            + [pltpu.SemaphoreType.DMA((3,))],
            cost_estimate=small,
            compiler_params=params,
            name="grads",
        )(*operands, *last)
        last = [grads[3]]
        return grads[:3]

    project(0, 0)
    project(1, 0)
    if far:
        project(far[0], 0)
    act(0, 0)
    act(1, 0)
    if far:
        project(far[0], 1)
    for i, z in enumerate(far):
        final = i + 1 == len(far)
        project(1 if final else far[i + 1], 1 if final else 0)
        act(z, 0)
        act(z, 1)
        project(0 if final else far[i + 1], 1)
        if i > 0:
            collect(far[i - 1])
        send_sum(z)
    if not far:
        project(1, 1)
        project(0, 1)
    act(1, 1)
    send_sum(1)
    act(0, 1)
    grad_gate, grad_up, grad_down = run_grads()
    last_terms = (*total, keeps[0], received[0], *(arrivals[z] for z in [*far[-1:], 1]))
    pieces = merge([[piece] for piece in last_terms], [rows] * 4)
    moved = [swap(pieces[i], i % 2, 2 * (i // 2)) if i else pieces[i] for i in range(4)]
    layer_out, d_tokens = pl.pallas_call(
        functools.partial(finish_kernel, 2),
        out_shape=(shape(rows, features),) * 2,
        in_specs=[vmem] * 4,
        out_specs=(vmem,) * 2,
        cost_estimate=small,
        compiler_params=little,
        name="finish",
    )(moved[0], moved[2], moved[1], moved[3])

    return (layer_out, d_tokens, grad_gate, grad_up, grad_down)


def slots(tokens, routes, gates, cotangent, w_gate, w_up, w_down):
    tok_rows, features = tokens.shape
    fanout = routes.shape[1]
    experts = lax.axis_size("expert")
    groups = lax.axis_size("dp")
    capacity = min(tok_rows, max(2, 2 * tok_rows * fanout // experts))
    assigned = tok_rows * fanout
    expert_ids = routes.reshape(assigned)
    onehot = (expert_ids[:, None] == jnp.arange(experts, dtype=jnp.int32)[None, :]).astype(
        jnp.float32
    )
    assign_iota = jnp.arange(assigned, dtype=jnp.int32)
    earlier = (assign_iota[:, None] > assign_iota[None, :]).astype(jnp.float32)
    prior_count = jnp.dot(earlier, onehot, precision=lax.Precision.HIGHEST)
    slot_index = jnp.sum(prior_count * onehot, axis=1).astype(jnp.int32)
    position = expert_ids * capacity + slot_index
    slot_map = (
        jnp.arange(experts * capacity, dtype=jnp.int32)[:, None] == position[None, :]
    ).astype(jnp.float32)
    token_owner = (
        assign_iota[:, None] // fanout == jnp.arange(tok_rows, dtype=jnp.int32)[None, :]
    ).astype(jnp.float32)
    dispatch = jnp.dot(slot_map, token_owner, precision=lax.Precision.HIGHEST)
    weighted = jnp.dot(
        slot_map, token_owner * gates.reshape(assigned)[:, None], precision=lax.Precision.HIGHEST
    )
    send_input = jnp.dot(
        dispatch.astype(jnp.bfloat16), tokens, preferred_element_type=jnp.float32
    ).astype(jnp.bfloat16)
    send_dout = jnp.dot(
        weighted, cotangent.astype(jnp.float32), precision=lax.Precision.HIGHEST
    ).astype(jnp.bfloat16)
    send_input = send_input.reshape(1, experts, capacity, features)
    send_dout = send_dout.reshape(1, experts, capacity, features)
    moved = (
        lax.all_to_all(send_input, "dp", split_axis=3, concat_axis=0, tiled=True),
        lax.all_to_all(send_dout, "dp", split_axis=3, concat_axis=0, tiled=True),
    )
    moved = (
        lax.all_to_all(moved[0], "expert", split_axis=1, concat_axis=1, tiled=True),
        lax.all_to_all(moved[1], "expert", split_axis=1, concat_axis=1, tiled=True),
    )
    part_width = moved[0].shape[3]
    total_rows = groups * experts * capacity
    input_rows = moved[0].reshape(total_rows, part_width)
    dout_rows = moved[1].reshape(total_rows, part_width)
    gate_local = w_gate[0]
    up_local = w_up[0]
    down_local = w_down[0]
    own_rows = total_rows // groups
    own_start = lax.axis_index("dp") * own_rows
    gate_part = jnp.dot(input_rows, gate_local, preferred_element_type=jnp.float32)
    up_part = jnp.dot(input_rows, up_local, preferred_element_type=jnp.float32)
    gate_all, up_all = (
        lax.psum(gate_part.astype(jnp.bfloat16), "dp").astype(jnp.float32),
        lax.psum(up_part.astype(jnp.bfloat16), "dp").astype(jnp.float32),
    )
    hidden = (jax.nn.silu(gate_all) * up_all).astype(jnp.bfloat16)
    gate_own = lax.dynamic_slice_in_dim(gate_all, own_start, own_rows, 0)
    up_own = lax.dynamic_slice_in_dim(up_all, own_start, own_rows, 0)
    out_slots = jnp.dot(hidden, down_local, preferred_element_type=jnp.float32).astype(jnp.bfloat16)
    grad_down = jnp.einsum(
        "rf,rd->fd", hidden, dout_rows, preferred_element_type=jnp.float32
    ).astype(jnp.bfloat16)
    dhidden_part = jnp.einsum(
        "rd,fd->rf", dout_rows, down_local, preferred_element_type=jnp.float32
    )
    dhidden_own = lax.psum_scatter(
        dhidden_part.astype(jnp.bfloat16), "dp", scatter_dimension=0, tiled=True
    ).astype(jnp.float32)
    sigmoid_gate = jax.nn.sigmoid(gate_own)
    silu_gate = gate_own * sigmoid_gate
    dgate_own = (
        dhidden_own * up_own * sigmoid_gate * (1.0 + gate_own * (1.0 - sigmoid_gate))
    ).astype(jnp.bfloat16)
    dup_own = (dhidden_own * silu_gate).astype(jnp.bfloat16)
    dgate_all, dup_all = (
        lax.all_gather(dgate_own, "dp", axis=0, tiled=True),
        lax.all_gather(dup_own, "dp", axis=0, tiled=True),
    )
    grad_gate = jnp.einsum(
        "rd,rf->df", input_rows, dgate_all, preferred_element_type=jnp.float32
    ).astype(jnp.bfloat16)
    grad_up = jnp.einsum(
        "rd,rf->df", input_rows, dup_all, preferred_element_type=jnp.float32
    ).astype(jnp.bfloat16)
    back_slots = (
        jnp.einsum("rf,df->rd", dgate_all, gate_local, preferred_element_type=jnp.float32)
        + jnp.einsum("rf,df->rd", dup_all, up_local, preferred_element_type=jnp.float32)
    ).astype(jnp.bfloat16)
    out_slots = out_slots.reshape(groups, experts, capacity, part_width)
    back_slots = back_slots.reshape(groups, experts, capacity, part_width)
    returned = (
        lax.all_to_all(out_slots, "expert", split_axis=1, concat_axis=1, tiled=True),
        lax.all_to_all(back_slots, "expert", split_axis=1, concat_axis=1, tiled=True),
    )
    returned = (
        lax.all_to_all(returned[0], "dp", split_axis=0, concat_axis=3, tiled=True),
        lax.all_to_all(returned[1], "dp", split_axis=0, concat_axis=3, tiled=True),
    )
    out_tokens = returned[0].reshape(experts * capacity, features)
    back_tokens = returned[1].reshape(experts * capacity, features)
    layer_out = jnp.dot(
        weighted.T, out_tokens.astype(jnp.float32), precision=lax.Precision.HIGHEST
    ).astype(jnp.bfloat16)
    d_tokens = jnp.dot(
        dispatch.T.astype(jnp.bfloat16), back_tokens, preferred_element_type=jnp.float32
    ).astype(jnp.bfloat16)
    return (layer_out, d_tokens, grad_gate[None], grad_up[None], grad_down[None])


def local(tokens, routes, gates, cotangent, w_gate, w_up, w_down):
    rows, fanout = routes.shape
    experts, groups = lax.axis_size("expert"), lax.axis_size("dp")
    capacity = min(rows, max(2, 2 * rows * fanout // experts))
    bits = experts & (experts - 1) == 0 and experts >= 8
    form = dense if capacity == rows and groups == 2 and bits else slots
    return form(tokens, routes, gates, cotangent, w_gate, w_up, w_down)


def solution(mesh):
    return jax.shard_map(
        local,
        mesh=mesh,
        in_specs=(
            P(("dp", "expert"), None),
            P(("dp", "expert"), None),
            P(("dp", "expert"), None),
            P(("dp", "expert"), None),
            P("expert", "dp", None),
            P("expert", "dp", None),
            P("expert", None, "dp"),
        ),
        out_specs=(
            P(("dp", "expert"), None),
            P(("dp", "expert"), None),
            P("expert", "dp", None),
            P("expert", "dp", None),
            P("expert", None, "dp"),
        ),
        check_vma=False,
    )
```

```python
import functools

import jax
import jax.numpy as jnp
from jax import lax
from jax.experimental import pallas as pl
from jax.experimental.pallas import tpu as pltpu
from jax.sharding import PartitionSpec as P


def swap(value, dp_bit, expert_bits):
    groups, experts = lax.axis_size("dp"), lax.axis_size("expert")
    if dp_bit == 0:
        pairs = [(e, e ^ expert_bits) for e in range(experts)]
        return lax.ppermute(value, "expert", pairs)
    pairs = [
        (d * experts + e, (d ^ dp_bit) * experts + (e ^ expert_bits))
        for d in range(groups)
        for e in range(experts)
    ]
    return lax.ppermute(value, ("dp", "expert"), pairs)


def prepare_kernel(tokens_ref, routes_ref, gates_ref, cotangent_ref, mine_ref, other_ref, *, experts, part):
    rows, fanout = tokens_ref.shape[0], routes_ref.shape[0]
    width = mine_ref.shape[1] - 2 * part
    routes, gates = routes_ref[...].T, gates_ref[...].T
    lane = lax.broadcasted_iota(jnp.int32, (rows, width), 1)
    named = lax.rem(lane, experts)
    table = jnp.zeros((rows, width), jnp.float32)
    for k in range(fanout):
        table = table + jnp.where(routes[:, k : k + 1] == named, gates[:, k : k + 1], 0.0)
    high = table.astype(jnp.bfloat16).astype(jnp.float32)
    middle = (table - high).astype(jnp.bfloat16).astype(jnp.float32)
    low = table - high - middle
    piece = lane // experts
    extra = jnp.where(piece == 0, high, jnp.where(piece == 1, middle, jnp.where(piece == 2, low, 0.0)))
    extra = extra.astype(jnp.bfloat16)
    dp_index = lax.axis_index("dp")
    for ref, owner in ((mine_ref, dp_index), (other_ref, 1 - dp_index)):
        columns = pl.ds(pl.multiple_of(owner * part, part), part)
        ref[:, :part] = tokens_ref[:, columns]
        ref[:, part : 2 * part] = cotangent_ref[:, columns]
        ref[:, 2 * part :] = extra


def begin(copies):
    for copy in copies:
        copy.start()
    return copies


def partial_kernel(count, parts, experts, part, *refs):
    f32, bf16 = jnp.float32, jnp.bfloat16
    pieces, weights = refs[:count], refs[count : count + 3]
    scale_ref, input_ref, dout_ref = refs[-3:]
    own_refs = refs[-3 - parts : -3]
    gate_ref, up_ref, down_ref = (weight.at[0] for weight in weights)
    units = gate_ref.shape[1]
    start = 0
    for piece in pieces:
        rows = piece.shape[0]
        here = slice(start, start + rows)
        start += rows
        extra = piece[:, 2 * part :].astype(f32)
        lane = lax.broadcasted_iota(jnp.int32, extra.shape, 1)
        scale = jnp.sum(
            jnp.where(lax.rem(lane, experts) == lax.axis_index("expert"), extra, 0.0), axis=1, keepdims=True
        )
        scale_ref[here, :] = jnp.broadcast_to(scale, (rows, scale_ref.shape[1]))
        input_ref[here, :] = piece[:, :part]
        dout_ref[here, :] = (scale * piece[:, part : 2 * part].astype(f32)).astype(bf16)
    def store(columns, value):
        start = 0
        for ref in own_refs:
            ref[:, columns] = value[start : start + ref.shape[0]].astype(bf16)
            start += ref.shape[0]

    for i, weight in enumerate((gate_ref, up_ref)):
        store(
            slice(i * units, (i + 1) * units),
            jnp.dot(input_ref[...], weight[...], preferred_element_type=f32),
        )
    across = (((1,), (1,)), ((), ()))
    store(
        slice(2 * units, 3 * units),
        lax.dot_general(dout_ref[...], down_ref[...], across, preferred_element_type=f32),
    )


def expert_kernel(block, skipped, parts, first, own_ref, their_ref, scale_ref, *refs):
    f32, bf16 = jnp.float32, jnp.bfloat16
    weights, refs = refs[:3], refs[3 + skipped :]
    pieces, refs = refs[:parts], refs[parts:]
    hidden_ref, dgate_ref, dup_ref = refs
    gate_ref, up_ref, down_ref = (weight.at[0] for weight in weights)
    rows = own_ref.shape[0]
    part, units = gate_ref.shape
    blocks = [their_ref[(i ^ 1) * block : ((i ^ 1) + 1) * block, :] for i in range(rows // block)]
    total = own_ref[...].astype(f32) + jnp.concatenate(blocks, axis=0).astype(f32)
    gate, up, dhidden = total[:, :units], total[:, units : 2 * units], total[:, 2 * units :]
    sigmoid = jax.nn.sigmoid(gate)
    silu = gate * sigmoid
    hidden_ref[...] = (silu * up).astype(bf16)
    dgate_ref[...] = (dhidden * up * sigmoid * (1.0 + gate * (1.0 - sigmoid))).astype(bf16)
    dup_ref[...] = (dhidden * silu).astype(bf16)
    half = rows // parts
    out = scale_ref[first : first + rows, :1] * jnp.dot(hidden_ref[...], down_ref[...], preferred_element_type=f32)
    for i, ref in enumerate(pieces):
        ref[:, :part] = out[i * half : (i + 1) * half].astype(bf16)
    across = (((1,), (1,)), ((), ()))
    back = lax.dot_general(dgate_ref[...], gate_ref[...], across, preferred_element_type=f32)
    back = back + lax.dot_general(dup_ref[...], up_ref[...], across, preferred_element_type=f32)
    for i, ref in enumerate(pieces):
        ref[:, part:] = back[i * half : (i + 1) * half].astype(bf16)


def merge_kernel(counts, parts, *refs):
    terms, first = [], 0
    for count in counts:
        group = refs[first : first + count]
        terms.append(jnp.concatenate([ref[...].astype(jnp.float32) for ref in group], axis=0))
        first += count
    total = sum(terms)
    start = 0
    for piece in refs[-parts:]:
        rows = piece.shape[0]
        piece[...] = total[start : start + rows].astype(piece.dtype)
        start += rows


def gather_kernel(count, parts, *refs):
    rows = jnp.concatenate([ref[...] for ref in refs[:count]], axis=0)
    start = 0
    for piece in refs[-parts:]:
        piece[...] = rows[start : start + piece.shape[0]]
        start += piece.shape[0]


def finish_kernel(count, *refs):
    f32 = jnp.float32
    out_ref, back_ref = refs[2 * count :]
    part = refs[0].shape[1] // 2
    dp_index = lax.axis_index("dp")
    for owner, terms in ((dp_index, refs[:count]), (1 - dp_index, refs[count : 2 * count])):
        columns = pl.ds(pl.multiple_of(owner * part, part), part)
        for ref, start in ((out_ref, 0), (back_ref, part)):
            total = sum(term[:, start : start + part].astype(f32) for term in terms)
            ref[:, columns] = total.astype(ref.dtype)


def grad_kernel(counts, *refs):
    bf16 = jnp.bfloat16
    groups, start = [], 0
    for count in counts:
        groups.append(refs[start : start + count])
        start += count
    outs, token_ref, results, done = refs[-8:-5], refs[-5], refs[-4:-1], refs[-1]
    token_ref[...] = jnp.zeros_like(token_ref)

    def rows_of(group):
        return jnp.concatenate([ref[...] for ref in group], axis=0)

    over_rows = (((0,), (0,)), ((), ()))
    copies = []
    for i, (left, right) in enumerate(((0, 3), (0, 4), (2, 1))):
        results[i][0] = lax.dot_general(
            rows_of(groups[left]),
            rows_of(groups[right]),
            over_rows,
            preferred_element_type=jnp.float32,
        ).astype(bf16)
        copies += begin([pltpu.make_async_copy(results[i], outs[i], done.at[i])])
    for copy in copies:
        copy.wait()


def dense(tokens, routes, gates, cotangent, w_gate, w_up, w_down):
    f32, bf16 = jnp.float32, jnp.bfloat16
    rows, features = tokens.shape
    experts = lax.axis_size("expert")
    part, units = w_gate.shape[1:]
    wide = 2 * part + -(-3 * experts // 128) * 128
    params = pltpu.CompilerParams(vmem_limit_bytes=20 * 1024 * 1024)
    little = pltpu.CompilerParams(vmem_limit_bytes=4 * 1024 * 1024)
    long = pl.CostEstimate(flops=int(1e10), bytes_accessed=1000, transcendentals=0)
    small = pl.CostEstimate(flops=1000, bytes_accessed=1000, transcendentals=0)
    vmem = pl.BlockSpec(memory_space=pltpu.VMEM)
    anywhere = pl.BlockSpec(memory_space=pl.ANY)

    def shape(*dims, dtype=bf16):
        return jax.ShapeDtypeStruct(dims, dtype)

    mine, other = pl.pallas_call(
        functools.partial(prepare_kernel, experts=experts, part=part),
        out_shape=(shape(rows, wide), shape(rows, wide)),
        in_specs=[vmem] * 4,
        out_specs=(vmem, vmem),
        cost_estimate=long,
        compiler_params=pltpu.CompilerParams(vmem_limit_bytes=55 * 1024 * 1024),
        name="prepare",
    )(tokens, routes.T, gates.T, cotangent)

    weights = (w_gate, w_up, w_down)
    last, kept = [], []

    def partials(pieces, sizes):
        nonlocal last
        count = sum(piece.shape[0] for piece in pieces)
        outs = pl.pallas_call(
            functools.partial(partial_kernel, len(pieces), len(sizes), experts, part),
            out_shape=tuple(shape(size, 3 * units) for size in sizes)
            + (shape(count, 128, dtype=f32), shape(count, part), shape(count, part)),
            in_specs=[vmem] * len(pieces) + [vmem] * (3 + len(last)),
            out_specs=(vmem,) * (len(sizes) + 3),
            cost_estimate=small,
            compiler_params=params,
            name="partials",
        )(*pieces, *weights, *last)
        last = [outs[len(sizes)]]
        return outs[: len(sizes)], outs[-3:]

    def expert(own, theirs, scale, first, parts):
        nonlocal last
        count = own.shape[0]
        outs = pl.pallas_call(
            functools.partial(expert_kernel, rows, len(last), parts, first),
            out_shape=(shape(count // parts, 2 * part),) * parts + (shape(count, units),) * 3,
            in_specs=[vmem] * 3 + [vmem] * (3 + len(last)),
            out_specs=(vmem,) * (parts + 3),
            cost_estimate=small,
            compiler_params=params,
            name="expert",
        )(own, theirs, scale, *weights, *last)
        last = [outs[0]]
        return outs[:parts], outs[parts:]

    def merge(terms, sizes):
        nonlocal last
        pieces = [piece for term in terms for piece in term]
        outs = pl.pallas_call(
            functools.partial(merge_kernel, [len(term) for term in terms], len(sizes)),
            out_shape=tuple(shape(size, pieces[0].shape[1]) for size in sizes),
            in_specs=[vmem] * (len(pieces) + len(last)),
            out_specs=(vmem,) * len(sizes),
            cost_estimate=small,
            compiler_params=little,
            name="merge",
        )(*pieces, *last)
        last = [outs[0]]
        return list(outs)

    def gather(pieces, sizes):
        nonlocal last
        outs = pl.pallas_call(
            functools.partial(gather_kernel, len(pieces), len(sizes)),
            out_shape=tuple(shape(size, pieces[0].shape[1]) for size in sizes),
            in_specs=[vmem] * (len(pieces) + len(last)),
            out_specs=(vmem,) * len(sizes),
            cost_estimate=small if last else long,
            compiler_params=little,
            name="gather",
        )(*pieces, *last)
        last = [outs[0]]
        return list(outs)

    planes = experts // 4
    far = list(range(planes - 1, 1, -1))
    half = 2 * rows
    [quad] = gather([mine, swap(other, 1, 0), swap(mine, 0, 2), swap(other, 1, 2)], [2 * half])
    quads = [quad] + [swap(quad, 0, 4 * z) for z in range(1, planes)]
    order, sent, saved, keeps, received, arrivals, total = [], {}, {}, {}, {}, {}, []

    def project(z, side):
        piece = swap(quads[z], 0, 1) if side else quads[z]
        [own], (scale, *rest) = partials([piece], [piece.shape[0]])
        sent[z, side] = (own, swap(own, 1, 0), scale)
        kept.append(rest)
        order.append((z, side))

    def act(z, side):
        [piece], saved[z, side] = expert(*sent[z, side], 0, 1)
        if side:
            received[z] = swap(piece, 0, 1)
        else:
            keeps[z] = piece

    def send_sum(z):
        [piece] = merge([[keeps[z]], [received[z]]], [2 * half])
        arrivals[z] = swap(piece, 0, 4 * z)

    def collect(z):
        total[:] = merge([[piece] for piece in total] + [[arrivals.pop(z)]], [2 * half])

    def run_grads():
        nonlocal last
        groups = [[arrays[i] for arrays in kept] for i in range(2)]
        groups += [[saved[key][i] for key in order] for i in range(3)]
        operands = [array for group in groups for array in group]
        grad_shapes = [(1, part, units), (1, part, units), (1, units, part)]
        grads = pl.pallas_call(
            functools.partial(grad_kernel, [len(group) for group in groups]),
            out_shape=tuple(shape(*dims) for dims in grad_shapes) + (shape(8, 128, dtype=f32),),
            in_specs=[vmem] * (len(operands) + len(last)),
            out_specs=(anywhere,) * 3 + (vmem,),
            scratch_shapes=[pltpu.VMEM(dims, bf16) for dims in grad_shapes]
            + [pltpu.SemaphoreType.DMA((3,))],
            cost_estimate=small,
            compiler_params=params,
            name="grads",
        )(*operands, *last)
        last = [grads[3]]
        return grads[:3]

    project(0, 0)
    project(1, 0)
    if far:
        project(far[0], 0)
    act(0, 0)
    act(1, 0)
    if far:
        project(far[0], 1)
    for i, z in enumerate(far):
        final = i + 1 == len(far)
        project(1 if final else far[i + 1], 1 if final else 0)
        act(z, 0)
        act(z, 1)
        project(0 if final else far[i + 1], 1)
        if i > 0:
            collect(far[i - 1])
        send_sum(z)
    if not far:
        project(1, 1)
        project(0, 1)
    act(1, 1)
    send_sum(1)
    act(0, 1)
    grad_gate, grad_up, grad_down = run_grads()
    last_terms = (*total, keeps[0], received[0], *(arrivals[z] for z in [*far[-1:], 1]))
    pieces = merge([[piece] for piece in last_terms], [rows] * 4)
    moved = [swap(pieces[i], i % 2, 2 * (i // 2)) if i else pieces[i] for i in range(4)]
    layer_out, d_tokens = pl.pallas_call(
        functools.partial(finish_kernel, 2),
        out_shape=(shape(rows, features),) * 2,
        in_specs=[vmem] * 4,
        out_specs=(vmem,) * 2,
        cost_estimate=small,
        compiler_params=little,
        name="finish",
    )(moved[0], moved[2], moved[1], moved[3])

    return (layer_out, d_tokens, grad_gate, grad_up, grad_down)


def slots(tokens, routes, gates, cotangent, w_gate, w_up, w_down):
    tok_rows, features = tokens.shape
    fanout = routes.shape[1]
    experts = lax.axis_size("expert")
    groups = lax.axis_size("dp")
    capacity = min(tok_rows, max(2, 2 * tok_rows * fanout // experts))
    assigned = tok_rows * fanout
    expert_ids = routes.reshape(assigned)
    onehot = (expert_ids[:, None] == jnp.arange(experts, dtype=jnp.int32)[None, :]).astype(
        jnp.float32
    )
    assign_iota = jnp.arange(assigned, dtype=jnp.int32)
    earlier = (assign_iota[:, None] > assign_iota[None, :]).astype(jnp.float32)
    prior_count = jnp.dot(earlier, onehot, precision=lax.Precision.HIGHEST)
    slot_index = jnp.sum(prior_count * onehot, axis=1).astype(jnp.int32)
    position = expert_ids * capacity + slot_index
    slot_map = (
        jnp.arange(experts * capacity, dtype=jnp.int32)[:, None] == position[None, :]
    ).astype(jnp.float32)
    token_owner = (
        assign_iota[:, None] // fanout == jnp.arange(tok_rows, dtype=jnp.int32)[None, :]
    ).astype(jnp.float32)
    dispatch = jnp.dot(slot_map, token_owner, precision=lax.Precision.HIGHEST)
    weighted = jnp.dot(
        slot_map, token_owner * gates.reshape(assigned)[:, None], precision=lax.Precision.HIGHEST
    )
    send_input = jnp.dot(
        dispatch.astype(jnp.bfloat16), tokens, preferred_element_type=jnp.float32
    ).astype(jnp.bfloat16)
    send_dout = jnp.dot(
        weighted, cotangent.astype(jnp.float32), precision=lax.Precision.HIGHEST
    ).astype(jnp.bfloat16)
    send_input = send_input.reshape(1, experts, capacity, features)
    send_dout = send_dout.reshape(1, experts, capacity, features)
    moved = (
        lax.all_to_all(send_input, "dp", split_axis=3, concat_axis=0, tiled=True),
        lax.all_to_all(send_dout, "dp", split_axis=3, concat_axis=0, tiled=True),
    )
    moved = (
        lax.all_to_all(moved[0], "expert", split_axis=1, concat_axis=1, tiled=True),
        lax.all_to_all(moved[1], "expert", split_axis=1, concat_axis=1, tiled=True),
    )
    part_width = moved[0].shape[3]
    total_rows = groups * experts * capacity
    input_rows = moved[0].reshape(total_rows, part_width)
    dout_rows = moved[1].reshape(total_rows, part_width)
    gate_local = w_gate[0]
    up_local = w_up[0]
    down_local = w_down[0]
    own_rows = total_rows // groups
    own_start = lax.axis_index("dp") * own_rows
    gate_part = jnp.dot(input_rows, gate_local, preferred_element_type=jnp.float32)
    up_part = jnp.dot(input_rows, up_local, preferred_element_type=jnp.float32)
    gate_all, up_all = (
        lax.psum(gate_part.astype(jnp.bfloat16), "dp").astype(jnp.float32),
        lax.psum(up_part.astype(jnp.bfloat16), "dp").astype(jnp.float32),
    )
    hidden = (jax.nn.silu(gate_all) * up_all).astype(jnp.bfloat16)
    gate_own = lax.dynamic_slice_in_dim(gate_all, own_start, own_rows, 0)
    up_own = lax.dynamic_slice_in_dim(up_all, own_start, own_rows, 0)
    out_slots = jnp.dot(hidden, down_local, preferred_element_type=jnp.float32).astype(jnp.bfloat16)
    grad_down = jnp.einsum(
        "rf,rd->fd", hidden, dout_rows, preferred_element_type=jnp.float32
    ).astype(jnp.bfloat16)
    dhidden_part = jnp.einsum(
        "rd,fd->rf", dout_rows, down_local, preferred_element_type=jnp.float32
    )
    dhidden_own = lax.psum_scatter(
        dhidden_part.astype(jnp.bfloat16), "dp", scatter_dimension=0, tiled=True
    ).astype(jnp.float32)
    sigmoid_gate = jax.nn.sigmoid(gate_own)
    silu_gate = gate_own * sigmoid_gate
    dgate_own = (
        dhidden_own * up_own * sigmoid_gate * (1.0 + gate_own * (1.0 - sigmoid_gate))
    ).astype(jnp.bfloat16)
    dup_own = (dhidden_own * silu_gate).astype(jnp.bfloat16)
    dgate_all, dup_all = (
        lax.all_gather(dgate_own, "dp", axis=0, tiled=True),
        lax.all_gather(dup_own, "dp", axis=0, tiled=True),
    )
    grad_gate = jnp.einsum(
        "rd,rf->df", input_rows, dgate_all, preferred_element_type=jnp.float32
    ).astype(jnp.bfloat16)
    grad_up = jnp.einsum(
        "rd,rf->df", input_rows, dup_all, preferred_element_type=jnp.float32
    ).astype(jnp.bfloat16)
    back_slots = (
        jnp.einsum("rf,df->rd", dgate_all, gate_local, preferred_element_type=jnp.float32)
        + jnp.einsum("rf,df->rd", dup_all, up_local, preferred_element_type=jnp.float32)
    ).astype(jnp.bfloat16)
    out_slots = out_slots.reshape(groups, experts, capacity, part_width)
    back_slots = back_slots.reshape(groups, experts, capacity, part_width)
    returned = (
        lax.all_to_all(out_slots, "expert", split_axis=1, concat_axis=1, tiled=True),
        lax.all_to_all(back_slots, "expert", split_axis=1, concat_axis=1, tiled=True),
    )
    returned = (
        lax.all_to_all(returned[0], "dp", split_axis=0, concat_axis=3, tiled=True),
        lax.all_to_all(returned[1], "dp", split_axis=0, concat_axis=3, tiled=True),
    )
    out_tokens = returned[0].reshape(experts * capacity, features)
    back_tokens = returned[1].reshape(experts * capacity, features)
    layer_out = jnp.dot(
        weighted.T, out_tokens.astype(jnp.float32), precision=lax.Precision.HIGHEST
    ).astype(jnp.bfloat16)
    d_tokens = jnp.dot(
        dispatch.T.astype(jnp.bfloat16), back_tokens, preferred_element_type=jnp.float32
    ).astype(jnp.bfloat16)
    return (layer_out, d_tokens, grad_gate[None], grad_up[None], grad_down[None])


def local(tokens, routes, gates, cotangent, w_gate, w_up, w_down):
    rows, fanout = routes.shape
    experts, groups = lax.axis_size("expert"), lax.axis_size("dp")
    capacity = min(rows, max(2, 2 * rows * fanout // experts))
    bits = experts & (experts - 1) == 0 and experts >= 8
    form = dense if capacity == rows and groups == 2 and bits else slots
    return form(tokens, routes, gates, cotangent, w_gate, w_up, w_down)


def solution(mesh):
    return jax.shard_map(
        local,
        mesh=mesh,
        in_specs=(
            P(("dp", "expert"), None),
            P(("dp", "expert"), None),
            P(("dp", "expert"), None),
            P(("dp", "expert"), None),
            P("expert", "dp", None),
            P("expert", "dp", None),
            P("expert", None, "dp"),
        ),
        out_specs=(
            P(("dp", "expert"), None),
            P(("dp", "expert"), None),
            P("expert", "dp", None),
            P("expert", "dp", None),
            P("expert", None, "dp"),
        ),
        check_vma=False,
    )
```
